32 devices in a mesh: dp: 16 (over z, y, core), tensor: 2 (over x).
Axes of the slice: x: 2, y: 2, z: 4, core: 2. Of those that a mesh axis runs over, the one named last changes fastest.
Arguments:
- tokens: bfloat16 [32768, 1024], P(('dp', 'tensor')), may hold values from -12 to 12
- query_matrix: bfloat16 [1024, 1024], P(None, 'tensor'), may hold values from -0.1875 to 0.1875
- key_weight: bfloat16 [1024, 1024], P(None, 'tensor'), may hold values from -0.1875 to 0.1875
- value_weight: bfloat16 [1024, 1024], P(None, 'tensor'), may hold values from -0.1875 to 0.1875
- gate_weight: bfloat16 [1024, 1024], P(None, 'tensor'), may hold values from -0.1875 to 0.1875
- out_weight: bfloat16 [1024, 1024], P('tensor'), may hold values from -0.1875 to 0.1875
- left_weight: bfloat16 [1024, 2816], P(None, 'tensor'), may hold values from -0.1875 to 0.1875
- right_weight: bfloat16 [1024, 2816], P(None, 'tensor'), may hold values from -0.1875 to 0.1875
- down_weight: bfloat16 [2816, 1024], P('tensor'), may hold values from -0.109375 to 0.109375
- cotangent: bfloat16 [32768, 1024], P(('dp', 'tensor')), may hold values from -6 to 6
Outputs:
- result: bfloat16 [32768, 1024], P(('dp', 'tensor'))
- tokens_grad: float32 [32768, 1024], P(('dp', 'tensor'))
- query_weight_grad: float32 [1024, 1024], P('dp', 'tensor')
- key_weight_grad: float32 [1024, 1024], P('dp', 'tensor')
- value_weight_grad: float32 [1024, 1024], P('dp', 'tensor')
- gate_matrix_gradient: float32 [1024, 1024], P('dp', 'tensor')
- out_weight_grad: float32 [1024, 1024], P('tensor', 'dp')
- left_weight_grad: float32 [1024, 2816], P('dp', 'tensor')
- right_weight_grad: float32 [1024, 2816], P('dp', 'tensor')
- down_weight_grad: float32 [2816, 1024], P('tensor', 'dp')
The draws below stay inside these ranges and needn't reach their ends.
All inputs are finite; a program needn't handle non-finite values.
Results may differ from the reference program's by a relative error of at most 0.015.
Values may be sent and summed in bfloat16 or wider, within the bound.
No kernel may reach another device: no remote copies, remote signals or barrier semaphores. Data moves between devices by JAX's collectives and lax.ppermute only.
A program may use at most 256 MiB of HBM per device.

```python
import math
import jax
import jax.numpy as jnp
from jax import lax

D = 1024
HEADS = 16
HEAD_DIM = 64
FF = 2816
SEQ_LEN = 2048
BLOCK = 512
TOKENS = 32768


def draw_tokens(key, part):
    key_base = jax.random.fold_in(key, 11)
    key_rows = jax.random.fold_in(key, 12)
    key_cols = jax.random.fold_in(key, 13)
    row_scale = jnp.exp(jax.random.uniform(key_rows, (TOKENS, 1), jnp.float32, math.log(0.5), math.log(2.0)))
    col_scale = jnp.exp(jax.random.uniform(key_cols, (1, D), jnp.float32, math.log(0.7), math.log(1.4)))
    base = jnp.clip(jax.random.normal(key_base, (TOKENS, D), jnp.float32), -4.0, 4.0)
    return (base * row_scale * col_scale).astype(jnp.bfloat16)


def spiked(entries, key, source, target, shards_of, factor):
    def block_of(axis_at):
        return (jnp.arange(entries.shape[axis_at]) // (entries.shape[axis_at] // shards_of)).reshape((-1,) + (1,) * (entries.ndim - 1 - axis_at))

    one_side = jax.random.permutation(key, shards_of)[block_of(target)]
    second = (block_of(target) + shards_of // 2) % shards_of
    return jnp.where((block_of(source) == one_side) | (block_of(source) == second), factor * entries, entries)


def block_levels(own_key, extent, split, least, largest):
    loudness, own = 1.0, jax.random.fold_in(own_key, 6)
    for position, shards_of in split:
        draws = jnp.exp(jax.random.uniform(jax.random.fold_in(own, position), (shards_of,), jnp.float32, least / len(split), largest / len(split)))
        loudness = loudness * jnp.repeat(draws, extent[position] // shards_of).reshape([-1 if axis == position else 1 for axis in range(len(extent))])
    return loudness


def bell_draw(stream_key, shape, deviation, reach, cuts=(), dtype=jnp.bfloat16):
    drawn = deviation * jax.random.normal(stream_key, shape, jnp.float32)
    if cuts:
        drawn = drawn * block_levels(stream_key, shape, cuts, -0.22, 0.18)
    return jnp.clip(drawn, -reach, reach).astype(dtype)


def noise_with(rng, extent, scale, limit, cuts, heavy, held_as=jnp.bfloat16):
    entries = scale * jax.random.normal(rng, extent, jnp.float32)
    if cuts:
        entries = entries * block_levels(rng, extent, cuts, -0.22, 0.18)
    return jnp.clip(spiked(entries, jax.random.fold_in(rng, 3), *heavy), -limit, limit).astype(held_as)


def setup_inputs(seed: int = 0) -> dict:
    arg_keys = jax.random.split(jax.random.key(seed), 11)
    tokens = draw_tokens(jax.random.fold_in(arg_keys[10], 71), 0)
    query_matrix = bell_draw(arg_keys[1], (D, D), D ** -0.5, 0.1875, ((1, 2),))
    key_weight = bell_draw(arg_keys[2], (D, D), D ** -0.5, 0.1875, ((1, 2),))
    value_weight = bell_draw(arg_keys[3], (D, D), D ** -0.5, 0.1875, ((1, 2),))
    gate_weight = bell_draw(arg_keys[4], (D, D), D ** -0.5, 0.1875, ((1, 2),))
    out_weight = bell_draw(arg_keys[5], (D, D), D ** -0.5, 0.1875, ((0, 2),))
    left_weight = bell_draw(arg_keys[6], (D, FF), D ** -0.5, 0.1875, ((1, 2),))
    right_weight = bell_draw(arg_keys[7], (D, FF), D ** -0.5, 0.1875, ((1, 2),))
    down_weight = bell_draw(arg_keys[8], (FF, D), FF ** -0.5, 0.109375, ((0, 2),))
    cotangent = noise_with(arg_keys[9], (TOKENS, D), 1.0, 6.0, ((0, 32),), (0, 1, 32, 2.75))
    return {"tokens": tokens, "query_matrix": query_matrix, "key_weight": key_weight, "value_weight": value_weight, "gate_weight": gate_weight, "out_weight": out_weight, "left_weight": left_weight, "right_weight": right_weight, "down_weight": down_weight, "cotangent": cotangent}


EPS = 1e-06

@jax.custom_vjp
def low(v):
    return lax.optimization_barrier(v.astype(jnp.bfloat16)).astype(jnp.float32)

@jax.custom_vjp
def low_back(v):
    return v

def low_keep(v):
    return (low(v), None)

def low_pass(kept, grad):
    return (grad,)

def back_keep(v):
    return (v, None)

def back_low(kept, grad):
    return (low(grad),)
low.defvjp(low_keep, low_pass)
low_back.defvjp(back_keep, back_low)

def highest(left_arg, right_arg):
    return jnp.dot(left_arg, right_arg, precision=lax.Precision.HIGHEST)

def simple_norm(values):
    return values * lax.rsqrt(lax.optimization_barrier(jnp.mean(values * values, axis=-1, keepdims=True)) + EPS)

def head_norm(values):
    return values * lax.rsqrt(jnp.maximum(lax.optimization_barrier(jnp.mean(values * values, axis=-1, keepdims=True)), 1.0))

def block_step(running_state, pieces):
    query_part, key_portion, value_portion = pieces
    causal = jnp.tril(jnp.ones((BLOCK, BLOCK), jnp.float32))
    scores = jnp.einsum('qhe,khe->hqk', query_part, key_portion, precision=lax.Precision.HIGHEST)
    weights_low = low(low_back(scores * causal))
    inside = jnp.einsum('hqk,khe->qhe', weights_low, value_portion, precision=lax.Precision.HIGHEST)
    carried = jnp.einsum('qhe,hef->qhf', query_part, running_state, precision=lax.Precision.HIGHEST)
    following_state = running_state + jnp.einsum('utz,utd->tzd', key_portion, value_portion, precision=lax.Precision.HIGHEST)
    return (following_state, inside + carried)

def attend(query_rows, key_rows, value_rows):

    def to_blocks(values):
        return values.reshape(SEQ_LEN // BLOCK, BLOCK, HEADS, HEAD_DIM)
    start_state = jnp.zeros((HEADS, HEAD_DIM, HEAD_DIM), jnp.float32)
    _, outputs = lax.scan(jax.checkpoint(block_step), start_state, (to_blocks(query_rows), to_blocks(key_rows), to_blocks(value_rows)))
    return outputs.reshape(SEQ_LEN, D)

def layer_forward(inputs, query_matrix, key_weight, value_weight, gate_weight, out_weight, left_weight, right_weight, down_weight):
    normed_low = low(simple_norm(inputs))
    query_rows = low(jax.nn.softplus(low_back(highest(normed_low, query_matrix))))
    key_rows = low(jax.nn.softplus(low_back(highest(normed_low, key_weight))))
    value_rows = low(low_back(highest(normed_low, value_weight)))
    gate_pre = low_back(highest(normed_low, gate_weight))
    attn = low_back(attend(query_rows, key_rows, value_rows))
    heads_view = attn.reshape(SEQ_LEN, HEADS, HEAD_DIM)
    normed_attn = head_norm(heads_view).reshape(SEQ_LEN, D)
    mixed_low = low(normed_attn * gate_pre)
    residual = inputs + low_back(highest(mixed_low, out_weight))
    normed_mid_low = low(simple_norm(residual))
    left_act = low_back(highest(normed_mid_low, left_weight))
    right_act = low_back(highest(normed_mid_low, right_weight))
    product_low = low(left_act * right_act)
    return residual + highest(product_low, down_weight)

def reference(tokens, query_matrix, key_weight, value_weight, gate_weight, out_weight, left_weight, right_weight, down_weight, cotangent):
    weights = (query_matrix.astype(jnp.float32), key_weight.astype(jnp.float32), value_weight.astype(jnp.float32), gate_weight.astype(jnp.float32), out_weight.astype(jnp.float32), left_weight.astype(jnp.float32), right_weight.astype(jnp.float32), down_weight.astype(jnp.float32))
    seq_count = TOKENS // SEQ_LEN
    inputs = tokens.astype(jnp.float32).reshape(seq_count, SEQ_LEN, D)
    grads_in = cotangent.astype(jnp.float32).reshape(seq_count, SEQ_LEN, D)

    def per_sequence(totals, pieces):
        seq_input, seq_grad = pieces
        output, pull = jax.vjp(layer_forward, seq_input, *weights)
        grads = pull(seq_grad)
        totals = tuple((total + grad for total, grad in zip(totals, grads[1:])))
        return (totals, (output, grads[0]))
    start = tuple((jnp.zeros_like(weight) for weight in weights))
    totals, (outputs, input_grads) = lax.scan(per_sequence, start, (inputs, grads_in))
    return (outputs.reshape(TOKENS, D).astype(jnp.bfloat16), input_grads.reshape(TOKENS, D), totals[0], totals[1], totals[2], totals[3], totals[4], totals[5], totals[6], totals[7])
```

```python
import jax
import jax.numpy as jnp
from jax import lax
from jax.sharding import PartitionSpec as P

HEADS = 16
HEAD_DIM = 64
SEQ_LEN = 2048
CHUNK = 256
EPS = 1e-06
AXES = ("dp", "tensor")
LOW = jnp.bfloat16
F32 = jnp.float32


def mm(a, b, dims, out=F32):
    return lax.dot_general(a, b, ((dims[0], dims[1]), ((), ())), preferred_element_type=F32).astype(out)


def nn(a, b):
    return mm(a, b, ((1,), (0,)))


def nt_(a, b):
    return mm(a, b, ((1,), (1,)))


def norm_rows(values):
    factor = lax.rsqrt(jnp.mean(values * values, axis=-1, keepdims=True) + EPS)
    return (values * factor, factor)


def norm_back(grad_rows, normed, factor):
    return factor * (grad_rows - normed * jnp.mean(grad_rows * normed, axis=-1, keepdims=True))


class Comm:
    def __init__(self):
        self.nt = lax.axis_size("tensor")
        self.nd = lax.axis_size("dp")
        self.t = lax.axis_index("tensor")
        self.d = lax.axis_index("dp")
        self.core = self.d % 2
        self.y = (self.d // 2) % 2
        self.bits = self.nd.bit_length() - 1

    def send(self, values, partner):
        pairs = []
        for d in range(self.nd):
            for t in range(self.nt):
                d2, t2 = partner(d, t)
                pairs.append((d * self.nt + t, d2 * self.nt + t2))
        return lax.ppermute(values, AXES, pairs)

    def over_x(self, values):
        return self.send(values, lambda d, t: (d, t ^ 1))

    def over_bit(self, values, bit):
        return self.send(values, lambda d, t: (d ^ (1 << bit), t))

    def first(self, values):
        return self.send(values, lambda d, t: (d ^ 2, t) if d & 1 else (d, t ^ 1))

    def second(self, values):
        return self.send(values, lambda d, t: (d, t ^ 1) if d & 1 else (d ^ 2, t))


def piece_rows(rows):
    shared = (6 * rows // 32 + 8) // 16 * 16
    return (rows - 2 * shared) // 4, shared


def fetch_other(c, arrays):
    one, two = [], []
    for a in arrays:
        p, s = piece_rows(a.shape[0])
        one.append(lax.dynamic_slice_in_dim(a, (2 * c.y + c.core) * p, p, 0))
        two.append(lax.dynamic_slice_in_dim(a, 4 * p + c.core * s, s, 0))
    one = c.over_x(jnp.concatenate(one, 0))
    two = c.over_x(jnp.concatenate(two, 0))
    one_y = c.over_bit(one, 1)
    one_c, one_yc, two_c = (c.over_bit(v, 0) for v in (one, one_y, two))
    outs = []
    at_p = at_s = 0
    for a in arrays:
        p, s = piece_rows(a.shape[0])
        full = jnp.zeros(a.shape, a.dtype)
        for block, yy, cc in (
            (one, c.y, c.core),
            (one_y, 1 - c.y, c.core),
            (one_c, c.y, 1 - c.core),
            (one_yc, 1 - c.y, 1 - c.core),
        ):
            full = lax.dynamic_update_slice_in_dim(full, block[at_p : at_p + p], (2 * yy + cc) * p, 0)
        for block, cc in ((two, c.core), (two_c, 1 - c.core)):
            full = lax.dynamic_update_slice_in_dim(full, block[at_s : at_s + s], 4 * p + cc * s, 0)
        at_p += p
        at_s += s
        outs.append(full)
    return outs


def relative_rows(c, values):
    rows, width = values.shape
    k = c.bits
    x = values.T.reshape((2,) * k + (width // c.nd, rows))
    for axis in range(k):
        bit = (c.d >> (k - 1 - axis)) % 2
        x = jnp.where(bit == 1, jnp.flip(x, axis), x)
    x = jnp.transpose(x, tuple(reversed(range(k))) + (k, k + 1))
    return x.reshape(width, rows)


def add(a, b, out=LOW):
    return (a.astype(F32) + b.astype(F32)).astype(out)


def reduce_grads(c, own, other):
    half = own.shape[0] // 2
    own_r = c.over_bit(own[half:], 0)
    other_r = c.over_bit(other[half:], 0)
    a0 = add(own[:half], own_r)
    a1 = add(other[:half], other_r)
    q = half // 2
    is0 = c.core == 0
    keep0, keep1 = a0[:q], jnp.where(is0, a0[q:], a1[:q])
    away = jnp.concatenate([jnp.where(is0, a1[:q], a0[q:]), a1[q:]], 0)
    got = c.first(away)
    b0, b1 = add(keep0, got[:q]), add(keep1, got[q:])
    total = add(b0, c.second(b1), F32 if c.bits == 2 else LOW)
    for bit in range(2, c.bits):
        h = total.shape[0] // 2
        total = add(total[:h], c.over_bit(total[h:], bit), F32 if bit == c.bits - 1 else LOW)
    return total


def split_chunks(v):
    rows, width = v.shape
    ch = min(CHUNK, rows)
    return v.reshape(rows // ch, ch, width // HEAD_DIM, HEAD_DIM)


def merge_chunks(v):
    return v.reshape(v.shape[0] * v.shape[1], -1)


def causal(n):
    return (lax.broadcasted_iota(jnp.int32, (n, n), 0) >= lax.broadcasted_iota(jnp.int32, (n, n), 1)).astype(F32)


def ein(spec, a, b):
    return jnp.einsum(spec, a, b, preferred_element_type=F32)


def exclusive(sums, reverse=False):
    run = jnp.cumsum(sums[::-1] if reverse else sums, axis=0)
    run = run[::-1] if reverse else run
    return run - sums


def attend_local(q, k, v):
    q, k, v = split_chunks(q), split_chunks(k), split_chunks(v)
    w = (ein("nqhe,nkhe->nhqk", q, k) * causal(q.shape[1])).astype(LOW)
    inside = ein("nhqk,nkhe->nqhe", w, v)
    sums = ein("nkhe,nkhf->nhef", k, v)
    states = exclusive(sums)
    carried = ein("nqhe,nhef->nqhf", q, states.astype(LOW))
    return merge_chunks(inside + carried), states, jnp.sum(sums, 0)


def attend_back(q, k, v, g, states, later):
    q, k, v, g = (split_chunks(a) for a in (q, k, v, g))
    mask = causal(q.shape[1])
    w = (ein("nqhe,nkhe->nhqk", q, k) * mask).astype(LOW)
    p = (ein("nqhe,nkhe->nhqk", g, v) * mask).astype(LOW)
    sums = ein("nqhe,nqhf->nhef", q, g)
    after = (exclusive(sums, True) + later).astype(LOW)
    states = states.astype(LOW)
    dq = ein("nhqk,nkhe->nqhe", p, k) + ein("nqhf,nhef->nqhe", g, states)
    dk = ein("nhqk,nqhe->nkhe", p, q) + ein("nkhf,nhef->nkhe", v, after)
    dv = ein("nhqk,nqhe->nkhe", w, g) + ein("nkhe,nhef->nkhf", k, after)
    return merge_chunks(dq), merge_chunks(dk), merge_chunks(dv)


def other_sums(c, sums, earlier):
    if c.nt == 2:
        got = c.over_x(sums.astype(LOW)).astype(F32)
        h = got.shape[0] // 2
        got = jnp.concatenate([got[h:], got[:h]], 0)
        return jnp.where(c.t == (1 if earlier else 0), got, 0.0)
    every = lax.all_gather(sums.astype(LOW), "tensor", axis=0).astype(F32)
    ids = lax.broadcasted_iota(jnp.int32, every.shape, 0)
    return jnp.sum(jnp.where(ids < c.t if earlier else ids > c.t, every, 0.0), axis=0)


def body(tokens, qw, kw, vw, gw, ow, lw, rw, dw, cot):
    c = Comm()
    rows = tokens.shape[0]
    if c.nt == 2:
        attn_w = [[qw, kw, vw, gw], fetch_other(c, [qw, kw, vw, gw])]
        ow2, dw2 = fetch_other(c, [ow, dw])
        lw2, rw2 = fetch_other(c, [lw, rw])
        out_w = [ow, ow2]
        ffn_w = [(lw, rw, dw), (lw2, rw2, dw2)]
    else:
        cols = lambda a: lax.all_gather(a, "tensor", axis=1, tiled=True)
        attn_w = [[cols(a) for a in (qw, kw, vw, gw)]]
        out_w = [lax.all_gather(ow, "tensor", axis=0, tiled=True)]
        ffn_w = [(cols(lw), cols(rw), lax.all_gather(dw, "tensor", axis=0, tiled=True))]
    parts = range(len(attn_w))

    inputs = tokens.astype(F32)
    normed_in, norm_in = norm_rows(inputs)
    low_in = normed_in.astype(LOW)
    low_in_t = relative_rows(c, low_in)
    cot_t = relative_rows(c, cot)

    q, k, v, gate, sq, sk, attn, states, sums = ([] for _ in range(9))
    for i in parts:
        w = attn_w[i]
        qp, kp = nn(low_in, w[0]), nn(low_in, w[1])
        q.append(jax.nn.softplus(qp).astype(LOW))
        k.append(jax.nn.softplus(kp).astype(LOW))
        sq.append(jax.nn.sigmoid(qp).astype(LOW))
        sk.append(jax.nn.sigmoid(kp).astype(LOW))
        v.append(nn(low_in, w[2]).astype(LOW))
        gate.append(nn(low_in, w[3]).astype(LOW))
        a, st, su = attend_local(q[i], k[i], v[i])
        attn.append(a)
        states.append(st)
        sums.append(su)
    before = other_sums(c, jnp.concatenate(sums, 0), True)
    branch = 0.0
    heads_each = HEADS // len(attn_w)
    normed, factor, mixed = [], [], []
    for i in parts:
        pre = before[i * heads_each : (i + 1) * heads_each]
        states[i] = states[i] + pre
        a = attn[i].reshape(rows, heads_each, HEAD_DIM)
        a = a + ein("qhe,hef->qhf", q[i].reshape(a.shape), pre.astype(LOW))
        ms = jnp.mean(a * a, axis=-1, keepdims=True)
        r = lax.rsqrt(jnp.maximum(ms, 1.0))
        factor.append((r, (ms > 1.0).astype(F32)))
        n = a * r
        normed.append(n)
        m = (n.reshape(rows, -1) * gate[i]).astype(LOW)
        mixed.append(m)
        branch = branch + nn(m, out_w[i])
    residual = inputs + branch
    normed_mid, norm_mid = norm_rows(residual)
    low_mid = normed_mid.astype(LOW)
    low_mid_t = relative_rows(c, low_mid)

    ffn_out = mid_grad = 0.0
    ffn_grads = []
    for i in parts:
        lwi, rwi, dwi = ffn_w[i]
        left, right = nn(low_mid, lwi), nn(low_mid, rwi)
        prod = (left * right).astype(LOW)
        ffn_out = ffn_out + nn(prod, dwi)
        pg = nt_(cot, dwi)
        ll, rl = (pg * right).astype(LOW), (pg * left).astype(LOW)
        mid_grad = mid_grad + nt_(ll, lwi) + nt_(rl, rwi)
        ffn_grads.append(tuple(mm(a, b, ((1,), (0,)), LOW) for a, b in ((cot_t, prod), (low_mid_t, ll), (low_mid_t, rl))))
    result = (residual + ffn_out).astype(LOW)
    resid_grad = cot.astype(F32) + norm_back(mid_grad, normed_mid, norm_mid)
    low_resid = resid_grad.astype(LOW)
    low_resid_t = relative_rows(c, low_resid)

    gate_low, attn_low, sums, out_grads, gate_grads = [], [], [], [], []
    for i in parts:
        mg = nt_(low_resid, out_w[i])
        shape = (rows, heads_each, HEAD_DIM)
        n = normed[i]
        gate_low.append((mg * n.reshape(rows, -1)).astype(LOW))
        m = (mg * gate[i]).reshape(shape)
        r, above = factor[i]
        al = (r * (m - above * n * jnp.mean(m * n, axis=-1, keepdims=True))).astype(LOW)
        attn_low.append(al.reshape(rows, -1))
        sums.append(ein("qhe,qhf->hef", q[i].reshape(shape), al))
        out_grads.append(mm(low_resid_t, mixed[i], ((1,), (0,)), LOW))
        gate_grads.append(mm(low_in_t, gate_low[i], ((1,), (0,)), LOW))
    later = other_sums(c, jnp.concatenate(sums, 0), False)
    in_grad = 0.0
    qkv_grads = []
    for i in parts:
        lat = later[i * heads_each : (i + 1) * heads_each]
        dq, dk, dv = attend_back(q[i], k[i], v[i], attn_low[i], states[i], lat)
        dq, dk, dv = (dq * sq[i]).astype(LOW), (dk * sk[i]).astype(LOW), dv.astype(LOW)
        qkv_grads.append(tuple(mm(low_in_t, d, ((1,), (0,)), LOW) for d in (dq, dk, dv)))
        for d, w in zip((dq, dk, dv, gate_low[i]), attn_w[i]):
            in_grad = in_grad + nt_(d, w)
    tokens_grad = resid_grad + norm_back(in_grad, normed_in, norm_in)

    if c.nt == 2:

        def reduced(groups):
            own, other = (jnp.concatenate(g, 1) for g in groups)
            total = reduce_grads(c, own, other)
            width = total.shape[1] // len(groups[0])
            return [total[:, j * width : (j + 1) * width] for j in range(len(groups[0]))]

    else:

        def reduced(groups):
            outs = []
            for g in groups[0]:
                width = g.shape[1] // c.nt
                x = lax.psum_scatter(g, "tensor", scatter_dimension=1, tiled=True)
                k_ = c.bits
                x = x.reshape((2,) * k_ + (x.shape[0] // c.nd, width))
                x = jnp.transpose(x, tuple(reversed(range(k_))) + (k_, k_ + 1))
                for axis in range(k_):
                    bit = (c.d >> (k_ - 1 - axis)) % 2
                    x = jnp.where(bit == 1, jnp.flip(x, axis), x)
                x = x.reshape(-1, width)
                outs.append(lax.psum_scatter(x, "dp", scatter_dimension=0, tiled=True).astype(F32))
            return outs

    down_g, left_g, right_g = reduced(ffn_grads)
    out_g, gate_g = reduced([(a, b) for a, b in zip(out_grads, gate_grads)])
    q_g, k_g, v_g = reduced(qkv_grads)
    return (result, tokens_grad, q_g, k_g, v_g, gate_g, out_g.T, left_g, right_g, down_g.T)


def solution(mesh):
    rows, cols = P(AXES, None), P(None, "tensor")
    lead = P("tensor", None)
    return jax.shard_map(
        body,
        mesh=mesh,
        in_specs=(rows, cols, cols, cols, cols, lead, cols, cols, lead, rows),
        out_specs=(
            rows,
            rows,
            P("dp", "tensor"),
            P("dp", "tensor"),
            P("dp", "tensor"),
            P("dp", "tensor"),
            P("tensor", "dp"),
            P("dp", "tensor"),
            P("dp", "tensor"),
            P("tensor", "dp"),
        ),
        check_vma=False,
    )
```

```python
import functools

import jax
import jax.numpy as jnp
from jax import lax
from jax.experimental import pallas as pl
from jax.experimental.pallas import tpu as pltpu
from jax.sharding import PartitionSpec as P

HEADS = 16
HEAD_DIM = 64
GROUP = 256
CHUNK = 256
EPS = 1e-06
AXES = ("dp", "tensor")
LOW = jnp.bfloat16
F32 = jnp.float32
SDS = jax.ShapeDtypeStruct
ANY = pl.BlockSpec(memory_space=pl.ANY)


def dot(a, b, ca, cb):
    return lax.dot_general(a, b, (((ca,), (cb,)), ((), ())), preferred_element_type=F32)


def params(mib=60):
    return pltpu.CompilerParams(vmem_limit_bytes=mib << 20)


def cost(flops, size):
    return pl.CostEstimate(flops=int(flops), bytes_accessed=int(size), transcendentals=0)


def whole(shape):
    return pl.BlockSpec(shape, lambda *_: (0,) * len(shape), pipeline_mode=pl.Buffered(1))


def iota(shape, axis):
    return lax.broadcasted_iota(jnp.int32, shape, axis)


def block_mask(dtype, value=1.0):
    same = (iota((GROUP, GROUP), 0) // HEAD_DIM) == (iota((GROUP, GROUP), 1) // HEAD_DIM)
    return jnp.where(same, value, 0.0).astype(dtype)


def head_row(h, dtype):
    return jnp.where(iota((1, GROUP), 1) // HEAD_DIM == h, 1.0, 0.0).astype(dtype)


def per_head(rows):
    return jnp.concatenate([rows * head_row(h, rows.dtype) for h in range(GROUP // HEAD_DIM)], axis=0)


def pick_heads(stacked):
    n = stacked.shape[0] // (GROUP // HEAD_DIM)
    out = stacked[:n] * head_row(0, F32)
    for h in range(1, GROUP // HEAD_DIM):
        out = out + stacked[h * n : (h + 1) * n] * head_row(h, F32)
    return out


def causal_low(stacked):
    n = stacked.shape[1]
    tri = jnp.where(iota((n, n), 0) >= iota((n, n), 1), 1.0, 0.0).astype(F32)
    parts = [stacked[h * n : (h + 1) * n] * tri for h in range(GROUP // HEAD_DIM)]
    return jnp.concatenate(parts, axis=0).astype(LOW)


def squeeze_state(s):
    out = s[:HEAD_DIM]
    for h in range(1, GROUP // HEAD_DIM):
        out = out + s[h * HEAD_DIM : (h + 1) * HEAD_DIM]
    return out


def spread_state(s, scale):
    return jnp.concatenate([s.astype(F32) * scale] * (GROUP // HEAD_DIM), axis=0) * block_mask(F32)


def head_mean(v, mean_low):
    return dot(v.astype(LOW), mean_low, 1, 0)


def softplus(v):
    return jnp.maximum(v, 0.0) + jnp.log1p(jnp.exp(-jnp.abs(v)))


def sigmoid_of_softplus(s):
    small = s * (1.0 - s * (0.5 - s * (1.0 / 6.0)))
    return jnp.where(s < 0.02, small, 1.0 - jnp.exp(-s))


def place_rows(src, natural, keep, away, blocks):
    size = natural.shape[0] // blocks
    for p in range(blocks):
        block = natural[pl.ds(pl.multiple_of(src[p] * size, size), size), :]
        ref, q = (keep, p) if p < blocks // 2 else (away, p - blocks // 2)
        ref[q * size : (q + 1) * size, :] = block


def norm_kernel(x, low):
    v = x[...].astype(F32)
    low[...] = (v * lax.rsqrt(jnp.mean(v * v, axis=-1, keepdims=True) + EPS)).astype(LOW)


def norm_low(x):
    rows, d = x.shape
    rb = min(256, rows)
    spec = pl.BlockSpec((rb, d), lambda i: (i, 0))
    return pl.pallas_call(
        norm_kernel, grid=(rows // rb,), in_specs=[spec], out_specs=spec, out_shape=SDS(x.shape, LOW), compiler_params=params(8)
    )(x)


def attend_kernel(n_kept, *refs):
    x, wq, wk, wv, wg = refs[:5]
    q, k, v, gate, attn, sums = refs[5 + n_kept : 11 + n_kept]
    q[...] = softplus(dot(x[...], wq[...], 1, 0)).astype(LOW)
    k[...] = softplus(dot(x[...], wk[...], 1, 0)).astype(LOW)
    v[...] = dot(x[...], wv[...], 1, 0).astype(LOW)
    gate[...] = dot(x[...], wg[...], 1, 0).astype(LOW)
    rows = x.shape[0]
    ch = min(CHUNK, rows)
    state = jnp.zeros((GROUP, GROUP), F32)
    mask = block_mask(F32)
    for c in range(rows // ch):
        at = slice(c * ch, (c + 1) * ch)
        qc, kc, vc = q[at, :], k[at, :], v[at, :]
        w = causal_low(dot(per_head(qc), kc, 1, 1))
        out = pick_heads(dot(w, vc, 1, 0))
        if c:
            out = out + dot(qc, state.astype(LOW), 1, 0)
        attn[at, :] = out
        state = state + dot(kc, vc, 0, 0) * mask
    sums[...] = squeeze_state(state).astype(LOW)


def attend(x, weights, at, kept):
    rows, d = x.shape
    groups = weights[0].shape[1] // GROUP
    w_spec = pl.BlockSpec((d, GROUP), lambda i: (0, i))
    col = pl.BlockSpec((rows, GROUP), lambda i: (0, at + i))
    shapes = [SDS((rows, d), LOW)] * 4 + [SDS((rows, d), F32), SDS((HEAD_DIM, d), LOW)]
    kept = list(kept or ())
    return pl.pallas_call(
        functools.partial(attend_kernel, len(kept)),
        grid=(groups,),
        in_specs=[whole((rows, d))] + [w_spec] * 4 + [ANY] * len(kept),
        out_specs=[col] * 5 + [pl.BlockSpec((HEAD_DIM, GROUP), lambda i: (0, at + i))],
        out_shape=shapes,
        input_output_aliases={5 + j: j for j in range(len(kept))},
        compiler_params=params(26),
        cost_estimate=cost(groups * (8 * rows * d * GROUP + 20 * rows * 256 * 256), 20 * rows * d),
    )(x, *weights, *kept)


def post_kernel(use, attn, q, gate, x, before, ow1, ow2, normed, factor, mixed, residual, mid):
    mean_low = block_mask(LOW, 1.0 / HEAD_DIM)
    for g in range(attn.shape[1] // GROUP):
        at = slice(g * GROUP, (g + 1) * GROUP)
        swapped = (g * GROUP + before.shape[1] // 2) % before.shape[1]
        state = spread_state(before[:, swapped : swapped + GROUP], use[0].astype(F32)).astype(LOW)
        a = attn[:, at] + dot(q[:, at], state, 1, 0)
        ms = head_mean(a * a, mean_low)
        r = lax.rsqrt(jnp.maximum(ms, 1.0))
        n = a * r
        normed[:, at] = n.astype(LOW)
        factor[:, at] = jnp.where(ms > 1.0, r, 2.0).astype(LOW)
        mixed[:, at] = (n * gate[:, at].astype(F32)).astype(LOW)
    half = ow1.shape[0]
    branch = dot(mixed[:, :half], ow1[...], 1, 0) + dot(mixed[:, half:], ow2[...], 1, 0)
    res = x[...].astype(F32) + branch
    residual[...] = res
    mid[...] = (res * lax.rsqrt(jnp.mean(res * res, axis=-1, keepdims=True) + EPS)).astype(LOW)


def post(use, attn, q, gate, x, before, ow1, ow2):
    rows, d = x.shape
    rb = min(256, rows)
    spec = pl.BlockSpec((rb, d), lambda i: (i, 0))
    return pl.pallas_call(
        post_kernel,
        grid=(rows // rb,),
        in_specs=[pl.BlockSpec(memory_space=pltpu.SMEM)] + [spec] * 4 + [whole(before.shape), whole(ow1.shape), whole(ow2.shape)],
        out_specs=[spec] * 5,
        out_shape=[SDS((rows, d), LOW)] * 3 + [SDS((rows, d), F32), SDS((rows, d), LOW)],
        compiler_params=params(24),
        cost_estimate=cost(2 * rows * d * d * 1.75, 24 * rows * d),
    )(use, attn, q, gate, x, before, ow1, ow2)


FT = 256


def ffn_kernel(front, more, last, blocks, src, mid, cot, *refs):
    la, lb, ra, rb, da, db = refs[:6]
    refs = refs[6:]
    if front:
        fronts, refs = refs[:6], refs[6:]
    if more:
        (ffn_in, grad_in), refs = refs[:2], refs[2:]
    if last:
        residual, refs = refs[0], refs[1:]
    (keep, away), refs = refs[:2], refs[2:]
    if last:
        (result, resid_grad, low_resid), refs = refs[:3], refs[3:]
    (ffn, grad), refs = refs[:2], refs[2:]
    mid_t, cot_t, w, dw, prod, lr, natural = refs
    i = pl.program_id(0)

    @pl.when(i == 0)
    def _():
        mid_t[...] = mid[...].T
        cot_t[...] = cot[...].T
        if more:
            ffn[...] = ffn_in[...]
            grad[...] = grad_in[...]
        else:
            ffn[...] = jnp.zeros_like(ffn)
            grad[...] = jnp.zeros_like(grad)

    def load(a, b, c, d, e, f):
        w[:, :128] = a[...]
        w[:, 128:FT] = b[...]
        w[:, FT : FT + 128] = c[...]
        w[:, FT + 128 :] = d[...]
        dw[:128, :] = e[...]
        dw[128:, :] = f[...]

    if front:

        @pl.when(i == 0)
        def _():
            load(*fronts)

        @pl.when(i > 0)
        def _():
            load(la, lb, ra, rb, da, db)

    else:
        load(la, lb, ra, rb, da, db)

    x = mid[...]
    left, right = dot(x, w[:, :FT], 1, 0), dot(x, w[:, FT:], 1, 0)
    back = dot(cot[...], dw[...], 1, 1)
    prod[...] = (left * right).astype(LOW)
    lr[:, :FT] = (back * right).astype(LOW)
    lr[:, FT:] = (back * left).astype(LOW)
    ffn[...] += dot(prod[...], dw[...], 1, 0)
    grad[...] += dot(lr[...], w[...], 1, 1)
    natural[:, :FT] = dot(cot_t[...], prod[...], 1, 0).astype(LOW)
    natural[:, FT:] = dot(mid_t[...], lr[...], 1, 0).astype(LOW)
    place_rows(src, natural, keep, away, blocks)

    if front:

        @pl.when(i == 0)
        def _():
            for ref in (keep, away):
                v = ref[...]
                parts = [v[:, m * FT + a * 128 : m * FT + a * 128 + 128] for a in range(2) for m in range(3)]
                for j, part in enumerate(parts):
                    ref[:, j * 128 : (j + 1) * 128] = part

    if last:

        @pl.when(i == pl.num_programs(0) - 1)
        def _():
            step = min(256, mid.shape[0])

            @pl.loop(0, mid.shape[0] // step)
            def _(j):
                at = pl.ds(pl.multiple_of(j * step, step), step)
                res = residual[at, :]
                result[at, :] = (res + ffn[at, :]).astype(LOW)
                f = lax.rsqrt(jnp.mean(res * res, axis=-1, keepdims=True) + EPS)
                n = res * f
                g = grad[at, :]
                g = cot[at, :].astype(F32) + f * (g - n * jnp.mean(g * n, axis=-1, keepdims=True))
                resid_grad[at, :] = g
                low_resid[at, :] = g.astype(LOW)


def ffn(src, blocks, mid, cot, weights, start, tiles, front=None, sums=None, residual=None):
    rows, d = mid.shape
    more, last = sums is not None, residual is not None
    back = 2 if front is not None else 0
    at = lambda k: lambda i: jnp.maximum(start + 2 * i + k - back, 0)
    col = lambda f: pl.BlockSpec((d, 128), lambda i, s: (0, f(i)))
    row = lambda f: pl.BlockSpec((128, d), lambda i, s: (f(i), 0))
    l, r, dn = weights
    ins = [mid, cot, l, l, r, r, dn, dn]
    specs = [whole((rows, d))] * 2 + [col(at(0)), col(at(1))] * 2 + [row(at(0)), row(at(1))]
    grads = [SDS((d // 2, tiles * 3 * FT), LOW)] * 2
    g_spec = pl.BlockSpec((d // 2, 3 * FT), lambda i, s: (0, i))
    scratch = [pltpu.VMEM((d, rows), LOW)] * 2 + [
        pltpu.VMEM((d, 2 * FT), LOW),
        pltpu.VMEM((FT, d), LOW),
        pltpu.VMEM((rows, FT), LOW),
        pltpu.VMEM((rows, 2 * FT), LOW),
        pltpu.VMEM((d, 3 * FT), LOW),
    ]
    wide = SDS((rows, d), F32)
    outs = [wide, wide]
    if front is not None:
        end = l.shape[1] // 128 - 1
        one_col = pl.BlockSpec((d, 128), lambda i, s: (0, end), pipeline_mode=pl.Buffered(1))
        one_row = pl.BlockSpec((128, d), lambda i, s: (end, 0), pipeline_mode=pl.Buffered(1))
        ins += [front[0], l, front[1], r, front[2], dn]
        specs += [one_col] * 4 + [one_row] * 2
    if more:
        ins += sums
        specs += [whole((rows, d))] * 2
    if last:
        ins += [residual]
        specs += [whole((rows, d))]
        outs = [SDS((rows, d), LOW), wide, SDS((rows, d), LOW)]
        scratch = [pltpu.VMEM((rows, d), F32)] * 2 + scratch
    return pl.pallas_call(
        functools.partial(ffn_kernel, front is not None, more, last, blocks),
        grid_spec=pltpu.PrefetchScalarGridSpec(
            num_scalar_prefetch=1,
            grid=(tiles,),
            in_specs=specs,
            out_specs=[g_spec, g_spec] + [whole((rows, d))] * len(outs),
            scratch_shapes=scratch,
        ),
        out_shape=grads + outs,
        compiler_params=params(54 if last else 40),
        cost_estimate=cost(18 * tiles * FT * rows * d, 20 * rows * d),
    )(src, *ins)


def back_kernel(resid, ow1, ow2, gate, normed, factor, q, gate_low, attn_low, sums, w):
    i = pl.program_id(0)
    half = pl.num_programs(0) // 2

    @pl.when(i < half)
    def _():
        w[...] = ow1[...]

    @pl.when(i >= half)
    def _():
        w[...] = ow2[...]

    mean_low = block_mask(LOW, 1.0 / HEAD_DIM)
    step = min(256, resid.shape[0])
    state = jnp.zeros((GROUP, GROUP), F32)
    for j in range(resid.shape[0] // step):
        at = slice(j * step, (j + 1) * step)
        mg = dot(resid[at, :], w[...], 1, 1)
        n = normed[at, :].astype(F32)
        gate_low[at, :] = (mg * n).astype(LOW)
        m = mg * gate[at, :].astype(F32)
        f = factor[at, :].astype(F32)
        above = f <= 1.0
        r = jnp.where(above, f, 1.0)
        al = (r * (m - jnp.where(above, n * head_mean(m * n, mean_low), 0.0))).astype(LOW)
        attn_low[at, :] = al
        state = state + dot(q[at, :], al, 0, 0)
    sums[...] = squeeze_state(state * block_mask(F32)).astype(LOW)


def back(resid, ow1, ow2, gate, normed, factor, q):
    rows, d = resid.shape
    groups = d // GROUP
    half = groups // 2
    col = pl.BlockSpec((rows, GROUP), lambda i: (0, i))
    return pl.pallas_call(
        back_kernel,
        grid=(groups,),
        in_specs=[
            whole((rows, d)),
            pl.BlockSpec((GROUP, d), lambda i: (jnp.minimum(i, half - 1), 0)),
            pl.BlockSpec((GROUP, d), lambda i: (jnp.maximum(i - half, 0), 0)),
        ]
        + [col] * 4,
        out_specs=[col, col, pl.BlockSpec((HEAD_DIM, GROUP), lambda i: (0, i))],
        out_shape=[SDS((rows, d), LOW)] * 2 + [SDS((HEAD_DIM, d), LOW)],
        scratch_shapes=[pltpu.VMEM((GROUP, d), LOW)],
        compiler_params=params(20),
        cost_estimate=cost(2.5 * rows * d * d, 14 * rows * d),
    )(resid, ow1, ow2, gate, normed, factor, q)


def side_kernel(blocks, src, resid, low_in, mixed, gate_low, keep, away, resid_t, in_t, natural):
    @pl.when(pl.program_id(0) == 0)
    def _():
        resid_t[...] = resid[...].T
        in_t[...] = low_in[...].T

    natural[:, :GROUP] = dot(resid_t[...], mixed[...], 1, 0).astype(LOW)
    natural[:, GROUP:] = dot(in_t[...], gate_low[...], 1, 0).astype(LOW)
    place_rows(src, natural, keep, away, blocks)


def side_grads(src, blocks, resid, low_in, mixed, gate_low):
    rows, d = resid.shape
    groups = d // GROUP
    col = pl.BlockSpec((rows, GROUP), lambda i, s: (0, i))
    out = pl.BlockSpec((d // 2, 2 * GROUP), lambda i, s: (0, i))
    return pl.pallas_call(
        functools.partial(side_kernel, blocks),
        grid_spec=pltpu.PrefetchScalarGridSpec(
            num_scalar_prefetch=1,
            grid=(groups,),
            in_specs=[whole((rows, d))] * 2 + [col] * 2,
            out_specs=[out, out],
            scratch_shapes=[pltpu.VMEM((d, rows), LOW)] * 2 + [pltpu.VMEM((d, 2 * GROUP), LOW)],
        ),
        out_shape=[SDS((d // 2, 2 * d), LOW)] * 2,
        compiler_params=params(20),
        cost_estimate=cost(4 * rows * d * d, 8 * rows * d + 4 * d * d),
    )(src, resid, low_in, mixed, gate_low)


def qkv_kernel(blocks, src, use, low_in, q, k, v, al, before, later, keep, away, dq, dk, dv, in_t, states, natural):
    @pl.when(pl.program_id(0) == 0)
    def _():
        in_t[...] = low_in[...].T

    rows = q.shape[0]
    ch = min(CHUNK, rows)
    chunks = rows // ch
    mask = block_mask(F32)
    state = spread_state(before[...], use[0].astype(F32))
    for c in range(chunks):
        at = slice(c * ch, (c + 1) * ch)
        states[c] = state.astype(LOW)
        if c < chunks - 1:
            state = state + dot(k[at, :], v[at, :], 0, 0) * mask
    after = spread_state(later[...], use[1].astype(F32))
    for c in reversed(range(chunks)):
        at = slice(c * ch, (c + 1) * ch)
        qc, kc, vc, ac = q[at, :], k[at, :], v[at, :], al[at, :]
        qs, acs = per_head(qc), per_head(ac)
        w = causal_low(dot(qs, kc, 1, 1))
        p = causal_low(dot(acs, vc, 1, 1))
        low = after.astype(LOW)
        g = pick_heads(dot(p, kc, 1, 0)) + dot(ac, states[c], 1, 1)
        dq[at, :] = (g * sigmoid_of_softplus(qc.astype(F32))).astype(LOW)
        g = dot(p, qs, 0, 0) + dot(vc, low, 1, 1)
        dk[at, :] = (g * sigmoid_of_softplus(kc.astype(F32))).astype(LOW)
        dv[at, :] = (dot(w, acs, 0, 0) + dot(kc, low, 1, 0)).astype(LOW)
        if c:
            after = after + dot(qc, ac, 0, 0) * mask
    for m, ref in enumerate((dq, dk, dv)):
        natural[:, m * GROUP : (m + 1) * GROUP] = dot(in_t[...], ref[...], 1, 0).astype(LOW)
    place_rows(src, natural, keep, away, blocks)


def qkv_grads(src, use, blocks, low_in, q, k, v, al, before, later):
    rows, d = low_in.shape
    groups = d // GROUP
    ch = min(CHUNK, rows)
    col = pl.BlockSpec((rows, GROUP), lambda i, *_: (0, i))
    state = pl.BlockSpec((HEAD_DIM, GROUP), lambda i, *_: (0, (i + groups // 2) % groups))
    out = pl.BlockSpec((d // 2, 3 * GROUP), lambda i, *_: (0, i))
    return pl.pallas_call(
        functools.partial(qkv_kernel, blocks),
        grid_spec=pltpu.PrefetchScalarGridSpec(
            num_scalar_prefetch=2,
            grid=(groups,),
            in_specs=[whole((rows, d))] + [col] * 4 + [state] * 2,
            out_specs=[out, out] + [col] * 3,
            scratch_shapes=[
                pltpu.VMEM((d, rows), LOW),
                pltpu.VMEM((rows // ch, GROUP, GROUP), LOW),
                pltpu.VMEM((d, 3 * GROUP), LOW),
            ],
        ),
        out_shape=[SDS((d // 2, 3 * d), LOW)] * 2 + [SDS((rows, d), LOW)] * 3,
        compiler_params=params(26),
        cost_estimate=cost(6 * rows * d * d + groups * 50 * rows * 256 * 256, 16 * rows * d + 6 * d * d),
    )(src, use, low_in, q, k, v, al, before, later)


def final_kernel(n, x, resid_grad, *refs):
    grads, weights, out = refs[:n], refs[n : 3 * n], refs[3 * n]
    total = 0.0
    for j, g in enumerate(grads):
        half = g.shape[1] // 2
        total = total + dot(g[:, :half], weights[2 * j][...], 1, 1) + dot(g[:, half:], weights[2 * j + 1][...], 1, 1)
    v = x[...].astype(F32)
    f = lax.rsqrt(jnp.mean(v * v, axis=-1, keepdims=True) + EPS)
    v = v * f
    out[...] = resid_grad[...] + f * (total - v * jnp.mean(total * v, axis=-1, keepdims=True))


def final(x, resid_grad, grads, weights):
    rows, d = x.shape
    rb = min(512, rows)
    spec = pl.BlockSpec((rb, d), lambda i: (i, 0))
    return pl.pallas_call(
        functools.partial(final_kernel, len(grads)),
        grid=(rows // rb,),
        in_specs=[spec] * (2 + len(grads)) + [whole(w.shape) for w in weights],
        out_specs=spec,
        out_shape=SDS((rows, d), F32),
        compiler_params=params(36),
        cost_estimate=cost(8 * rows * d * d, 16 * rows * d + 8 * d * d),
    )(x, resid_grad, *grads, *weights)


class Comm:
    def __init__(self):
        self.nt = lax.axis_size("tensor")
        self.nd = lax.axis_size("dp")
        self.t = lax.axis_index("tensor")
        self.d = lax.axis_index("dp")
        self.core = self.d % 2
        self.y = (self.d // 2) % 2
        self.bits = self.nd.bit_length() - 1
        z = (self.d // 4) % 2
        piece = lambda cc, y, zz: 4 * (cc % 2) + 2 * (y % 2) + zz % 2
        spots = []
        for cc in (self.core, self.core + 1):
            y = self.y
            spots += [piece(cc, y, z), piece(cc, y + 1, z + 1), piece(cc, y + 1, z), piece(cc, y, z + 1)]
        self.spots = jnp.stack(spots).astype(jnp.int32)

    def send(self, values, partner):
        pairs = []
        for d in range(self.nd):
            for t in range(self.nt):
                d2, t2 = partner(d, t)
                pairs.append((d * self.nt + t, d2 * self.nt + t2))
        return lax.ppermute(values, AXES, pairs)

    def over_x(self, values):
        return self.send(values, lambda d, t: (d, t ^ 1))

    def over_bit(self, values, bit):
        return self.send(values, lambda d, t: (d ^ (1 << bit), t))

    def first(self, values):
        return self.send(values, lambda d, t: (d ^ 2, t) if d & 1 else (d, t ^ 1))

    def second(self, values):
        return self.send(values, lambda d, t: (d, t ^ 1) if d & 1 else (d ^ 2, t))

    def sources(self):
        src = jnp.arange(self.nd, dtype=jnp.int32)
        rev = jnp.zeros_like(src)
        for b in range(self.bits):
            rev = rev + ((src >> b) % 2) * (1 << (self.bits - 1 - b))
        return jnp.bitwise_xor(rev, self.d.astype(jnp.int32))


def copy_all(copies, sems):
    started = [pltpu.make_async_copy(a, b, sems.at[j]) for j, (a, b) in enumerate(copies)]
    for s in started:
        s.start()
    for s in started:
        s.wait()


def pack_kernel(n, spots, *refs):
    arrays, (one, two) = refs[: 2 * n], refs[2 * n :]
    for out, parts in ((one, arrays[:n]), (two, arrays[n:])):
        at = 0
        for a in parts:
            out[at : at + a.shape[0], :] = a[...]
            at += a.shape[0]


def views(arrays):
    cols = min(a.shape[1] for a in arrays)
    return cols, [(i, h) for i, a in enumerate(arrays) for h in range(a.shape[1] // cols)]


def pack(spots, arrays):
    cols, blocks = views(arrays)
    rows = sum(arrays[i].shape[0] for i, _ in blocks) // 8
    specs = [
        pl.BlockSpec((arrays[i].shape[0] // 8, cols), lambda _, s, j=j, h=h: (s[j], h)) for j in range(2) for i, h in blocks
    ]
    return pl.pallas_call(
        functools.partial(pack_kernel, len(blocks)),
        grid_spec=pltpu.PrefetchScalarGridSpec(
            num_scalar_prefetch=1, grid=(1,), in_specs=specs, out_specs=[pl.BlockSpec((rows, cols), lambda i, s: (0, 0))] * 2
        ),
        out_shape=[SDS((rows, cols), LOW)] * 2,
        compiler_params=params(8),
        cost_estimate=cost(0, 8 * rows * cols),
    )(spots, *([arrays[i] for i, _ in blocks] * 2))


def unpack_kernel(where, n, spots, *refs):
    pieces, arrays, sems = refs[:8], refs[8 : 8 + n], refs[8 + n]
    cols = pieces[0].shape[1]
    at = 0
    copies = []
    for i, h in where:
        a = arrays[i]
        p = a.shape[0] // 8
        for j, piece in enumerate(pieces):
            to = a.at[pl.ds(pl.multiple_of(spots[j] * p, 16), p), pl.ds(h * cols, cols)]
            copies.append((piece.at[pl.ds(at, p)], to))
        at += p
    copy_all(copies, sems)


def unpack(spots, pieces, arrays):
    n = len(arrays)
    _, where = views(arrays)
    size = 2 * sum(a.size for a in arrays)
    return pl.pallas_call(
        functools.partial(unpack_kernel, where, n),
        grid_spec=pltpu.PrefetchScalarGridSpec(
            num_scalar_prefetch=1,
            grid=(1,),
            in_specs=[whole(b.shape) for b in pieces],
            out_specs=[ANY] * n,
            scratch_shapes=[pltpu.SemaphoreType.DMA((8 * len(where),))],
        ),
        out_shape=[SDS(a.shape, a.dtype) for a in arrays],
        compiler_params=params(12),
        cost_estimate=cost(0, 2 * size),
    )(spots, *pieces)


class Fetch:
    def __init__(self, c, arrays):
        self.c, self.arrays = c, arrays
        self.packed = pack(c.spots, arrays)

    def over_x(self, which, *others):
        return self.c.over_x(tie(self.packed[which], *others) if others else self.packed[which])

    def share(self, *others):
        one = tie(self.one, *others) if others else self.one
        self.mine = [self.one, self.two, self.c.over_bit(one, 1), self.c.over_bit(one, 2)]

    def cross(self, *others):
        mine = tie(self.mine, *others) if others else self.mine
        self.pieces = mine + [self.c.over_bit(b, 0) for b in mine]

    def get(self):
        return unpack(self.c.spots, self.pieces, self.arrays)


def tie(values, *others):
    return lax.optimization_barrier((values, others))[0]


def add(a, b, out=LOW):
    return (a.astype(F32) + b.astype(F32)).astype(out)


def quarter_kernel(front, core, *refs):
    own_k, own_r, oth_k, oth_r = refs[:4]
    refs = refs[4:]
    if front:
        f_k, f_r = refs[:2]
        refs = refs[2:]
    keep, away = refs[:2]
    h = own_k.shape[0] // 2
    own = add(own_k[...], own_r[...])
    if front:
        own = jnp.where(pl.program_id(0) == 0, add(f_k[...], f_r[...]), own)
    oth = add(oth_k[...], oth_r[...])
    keep[0] = own[:h]
    away[1] = oth[h:]

    @pl.when(core[0] == 0)
    def _():
        keep[1] = own[h:]
        away[0] = oth[:h]

    @pl.when(core[0] != 0)
    def _():
        keep[1] = oth[:h]
        away[0] = own[h:]


def quarters(core, own, own_at, oth, oth_at, tile, tiles, front=None):
    h = own[0].shape[0]
    at = lambda f: pl.BlockSpec((h, tile), lambda j, s: (0, f(j)))
    own_spec, oth_spec = at(own_at), at(oth_at)
    ins, specs = [*own, *oth], [own_spec] * 2 + [oth_spec] * 2
    if front is not None:
        ins += front
        specs += [at(lambda j: 0)] * 2
    out = pl.BlockSpec((2, h // 2, tile), lambda j, s: (0, 0, j))
    return pl.pallas_call(
        functools.partial(quarter_kernel, front is not None),
        grid_spec=pltpu.PrefetchScalarGridSpec(num_scalar_prefetch=1, grid=(tiles,), in_specs=specs, out_specs=[out, out]),
        out_shape=[SDS((2, h // 2, tile * tiles), LOW)] * 2,
        compiler_params=params(12),
        cost_estimate=cost(0, 12 * h * tile * tiles),
    )(core, *ins)


class Sum:
    def __init__(self, c, stay, leave):
        self.c, self.stay, self.leave, self.bit = c, stay, leave, 2
        self.got = c.first(leave)

    def step(self, *others):
        c = self.c
        got = tie(self.got, *others) if others else self.got
        if self.bit == 2:
            stay, leave = add(self.stay[0], got[0]), add(self.stay[1], got[1])
            self.total, self.leave, self.got = stay, leave, c.second(leave)
        elif self.bit <= c.bits:
            total = add(self.total, got)
            h = total.shape[0] // 2
            self.total, self.leave = total[:h], total[h:]
            self.got = c.over_bit(self.leave, self.bit - 1)
        else:
            self.total = add(self.total, got, F32)
        self.bit += 1
        return self

    def done(self):
        while self.bit <= self.c.bits + 1:
            self.step()
        return self.total


def untile(grads, n, width, front=0):
    outs = []
    for m in range(n):
        parts = [grads[:, m * front : (m + 1) * front]] if front else []
        parts += [grads[:, at + m * width : at + (m + 1) * width] for at in range(n * front, grads.shape[1], n * width)]
        outs.append(jnp.concatenate(parts, axis=1))
    return outs


def other_sums(c, sums, earlier):
    if c.nt == 2:
        return c.over_x(sums)
    every = lax.all_gather(sums, "tensor", axis=0).astype(F32)
    ids = iota(every.shape, 0)
    out = jnp.sum(jnp.where(ids < c.t if earlier else ids > c.t, every, 0.0), axis=0).astype(LOW)
    return jnp.roll(out, out.shape[1] // 2, 1)


def scatter_all(c, grads, src):
    d, cols = grads.shape
    blocks = jnp.zeros((c.nd, d // c.nd, cols), LOW).at[src].set(grads.reshape(c.nd, d // c.nd, cols))
    out = lax.psum_scatter(blocks.reshape(d, cols), "tensor", scatter_dimension=1, tiled=True)
    return lax.psum_scatter(out, "dp", scatter_dimension=0, tiled=True).astype(F32)


def body(tokens, qw, kw, vw, gw, ow, lw, rw, dw, cot):
    c = Comm()
    src = c.sources()
    core = c.core.astype(jnp.int32).reshape(1)
    use = jnp.stack([c.t > 0, c.t < c.nt - 1]).astype(jnp.int32) if c.nt == 2 else jnp.ones((2,), jnp.int32)
    own_w = [qw, kw, vw, gw]
    two = c.nt == 2
    if two:
        f1 = Fetch(c, own_w + [ow])
        f1.one, f1.two = f1.over_x(0), f1.over_x(1)
        low_in = norm_low(tokens)
        f2, f3 = Fetch(c, tie([lw, rw], f1.packed, low_in)), Fetch(c, tie([dw], f1.packed, low_in))
        f2.one, f3.one = f2.over_x(0), f3.over_x(0)
        f1.share()
        low_in = tie(low_in, f1.one, f2.packed, f3.packed)
    else:

        def halves(a, axis):
            full = lax.all_gather(a, "tensor", axis=axis, tiled=True)
            return jnp.split(full, 2, axis=axis)

        both = [halves(a, 1) for a in own_w]
        own_w, oth_w = [b[0] for b in both], [b[1] for b in both]
        (lw, lw2), (rw, rw2) = halves(lw, 1), halves(rw, 1)
        (ow, ow2), (dw, dw2) = halves(ow, 0), halves(dw, 0)
        low_in = norm_low(tokens)

    half = own_w[0].shape[1] // GROUP
    kept = attend(low_in, own_w, 0, None)
    if two:
        f1.cross(kept[0])
        *oth_w, ow2 = f1.get()
    q, k, v, gate, attn, sums = attend(low_in, oth_w, half, kept)
    before = other_sums(c, sums, True)
    if two:
        f2.two, f3.two = f2.over_x(1, before), f3.over_x(1, before)
        f2.share(sums)
        f3.share(sums)
        before = tie(before, f2.mine[0], f3.mine[0])
    normed, factor, mixed, residual, mid = post(use, attn, q, gate, tokens, before, ow, ow2)

    own = (lw, rw, dw)
    n_own = lw.shape[1] // FT
    n_two = n_own // 2
    n_three = n_own - n_two
    keep1, away1, *parts = ffn(src, c.nd, mid, cot, own, 0, n_own)
    over = lambda a: c.over_bit(a, 0) if two else a
    got1 = over(away1)
    if two:
        f2.cross(parts[0])
        f3.cross(parts[0])
        lw2, rw2 = f2.get()
        (dw2,) = f3.get()
    oth = (lw2, rw2, dw2)
    keep2, away2, *parts = ffn(src, c.nd, mid, cot, oth, 0, n_two + 1, own, parts)
    got2 = over(away2)
    tile = 384
    if two:
        pair, own_g = (keep2, got2), (keep1, got1)
        sum1 = Sum(
            c, *quarters(core, own_g, lambda j: jnp.maximum(j - 1, 0), pair, lambda j: j + 1, tile, 2 * n_two + 1, pair)
        )
        parts = tie(parts, sum1.leave)
    keep3, away3, result, resid_grad, resid = ffn(
        src, c.nd, mid, cot, oth, 2 * n_two, n_three, None, parts, residual
    )
    got3 = over(away3)
    if two:
        sum1.step(resid)
        resid = tie(resid, sum1.leave)
    gate_low, attn_low, sums = back(resid, ow, ow2, gate, normed, factor, q)
    later = other_sums(c, sums, False)
    if two:
        pair = (keep3, tie(got3, sums))
        stay, leave = quarters(core, own_g, lambda j: j + 2 * n_two, pair, lambda j: j, tile, 2 * n_three)
        sum2 = Sum(c, stay, tie(leave, later))
        sum1.step(sums, sum2.leave)
        gate_low = tie(gate_low, sum2.leave, sum1.leave)
    keep4, away4 = side_grads(src, c.nd, resid, low_in, mixed, gate_low)
    got4 = over(away4)
    if two:
        sum1.step(keep4)
        attn_low = tie(attn_low, sum1.leave, keep4)
    keep5, away5, dq, dk, dv = qkv_grads(src, use, c.nd, low_in, q, k, v, attn_low, before, later)
    got5 = over(away5)
    if two:
        sum2.step(dq)
        pair = (keep4, tie(got4, sum2.leave))
        sum4 = Sum(c, *quarters(core, pair, lambda j: j, pair, lambda j: j + half, 2 * GROUP, half))
        pair = (keep5, tie(got5, sum4.leave))
        sum5 = Sum(c, *quarters(core, pair, lambda j: j, pair, lambda j: j + half, 3 * GROUP, half))
        dq = tie(dq, sum5.leave)
    weights = [w for pair in zip(own_w, oth_w) for w in pair]
    tokens_grad = final(tokens, resid_grad, (dq, dk, dv, gate_low), weights)

    if two:
        part1, part2 = sum1.done(), sum2.done()
        out_g, gate_g = untile(sum4.done(), 2, GROUP)
        q_g, k_g, v_g = untile(sum5.done(), 3, GROUP)
        join = lambda one, two: [
            jnp.concatenate([a[:, 128:], b, a[:, :128]], 1) for a, b in zip(untile(one, 3, FT, 128), untile(two, 3, FT))
        ]
        down_g, left_g, right_g = join(part1, part2)
    else:
        rows_of = lambda a, b: jnp.concatenate([a, b], 0)
        g1, g2, g3 = rows_of(keep1, away1), rows_of(keep2, away2), rows_of(keep3, away3)
        own_g = [jnp.concatenate([a, b], 1) for a, b in zip(untile(g1, 3, FT), untile(g2[:, :384], 3, 128))]
        oth_g = untile(jnp.concatenate([g2[:, 768:], g3], 1), 3, FT)
        oth_g = [jnp.concatenate([a, b], 1) for a, b in zip(oth_g, untile(g2[:, 384:768], 3, 128))]
        down_g, left_g, right_g = (scatter_all(c, jnp.concatenate(p, 1), src) for p in zip(own_g, oth_g))
        out_g, gate_g = (scatter_all(c, g, src) for g in untile(rows_of(keep4, away4), 2, GROUP))
        q_g, k_g, v_g = (scatter_all(c, g, src) for g in untile(rows_of(keep5, away5), 3, GROUP))
    return (result, tokens_grad, q_g, k_g, v_g, gate_g, out_g.T, left_g, right_g, down_g.T)


def solution(mesh):
    rows, cols = P(AXES, None), P(None, "tensor")
    lead = P("tensor", None)
    return jax.shard_map(
        body,
        mesh=mesh,
        in_specs=(rows, cols, cols, cols, cols, lead, cols, cols, lead, rows),
        out_specs=(
            rows,
            rows,
            P("dp", "tensor"),
            P("dp", "tensor"),
            P("dp", "tensor"),
            P("dp", "tensor"),
            P("tensor", "dp"),
            P("dp", "tensor"),
            P("dp", "tensor"),
            P("tensor", "dp"),
        ),
        check_vma=False,
    )
```
